32 devices in a mesh: rcpt: 16 (over z, y, core), lon: 2 (over x).
Axes of the slice: x: 2, y: 2, z: 4, core: 2. Of those that a mesh axis runs over, the one named last changes fastest.
Arguments:
- adjoint_in: float32 [16, 4, 32, 16, 128], P('rcpt', None, 'lon'), may hold values from -6 to 6
- courants: float32 [16, 3, 32, 16, 128], P('rcpt', None, 'lon'), may hold values from -0.45 to 0.45
- owner: int32 [2], P('lon'), may hold values from 0 to 15
- rcpt_cell: int32 [16, 512], P('rcpt'), may hold values from 0 to 65535
- rcpt_hour: int32 [16, 512], P('rcpt'), may hold values from 0 to 2
- forcing: float32 [16, 4, 512], P('rcpt'), may hold values from -24 to 24
Outputs:
- adjoint_out: float32 [16, 4, 32, 16, 128], P('rcpt', None, 'lon')
The draws below stay inside these ranges and needn't reach their ends.
Inputs may be any that keep to these rules, and one draw needn't show every extreme that they name: `owner`: each band's met is read from one receptor row's slot. `rcpt_cell`: flat index (longitude * 16 + level) * 128 + latitude; several receptors may share a cell.
All inputs are finite; a program needn't handle non-finite values.
Results may differ from the reference program's by a relative error of at most 0.0003.
Values sent between devices are 32-bit elements; how exact they have to be, the bound alone decides.
A program may use at most 192 MiB of HBM per device.

```python
import jax
import jax.numpy as jnp
from jax import lax

STEPS = 3
TRACERS = 4
LON_DEV = 16
LEV = 16
LAT = 128
RECS = 512
BATCHES = 16
NLON = 32
N_RCPT = 16
N_LON = 2


def set_ends(values, stream_key, low, top_value):
    longest = values.shape.index(max(values.shape))
    spots = []
    for shift in (0, 1):
        where = [jax.random.randint(jax.random.fold_in(stream_key, axis), (), 0, length) for axis, length in enumerate(values.shape)]
        where[longest] = (where[longest] + shift) % values.shape[longest]
        spots.append(tuple(where))
    return values.at[spots[0]].set(low).at[spots[1]].set(top_value)


def steps_of(key, dims, pieces, smallest, high):
    factor_of = 1.0
    for dim, blocks in pieces:
        steps = jax.random.uniform(jax.random.fold_in(jax.random.fold_in(key, 6), dim), (blocks,), jnp.float32, smallest / len(pieces), high / len(pieces))
        factor_of = factor_of * jnp.repeat(jnp.exp(steps), dims[dim] // blocks).reshape((-1,) + (1,) * (len(dims) - 1 - dim))
    return factor_of


def bell_draw(stream_key, extent, width, reach, split=(), kind=jnp.bfloat16):
    gain = steps_of(stream_key, extent, split, -0.22, 0.18) if split else 1.0
    array = jax.random.normal(stream_key, extent, jnp.float32) * width * gain
    return jnp.minimum(jnp.maximum(array, -reach), reach).astype(kind)


def setup_inputs(seed: int = 0) -> dict:
    key_of = jax.random.split(jax.random.key(seed), 7)
    return {
        "adjoint_in": bell_draw(key_of[0], (BATCHES, TRACERS, NLON, LEV, LAT), 1.0, 6.0, ((0, 16), (2, 2)), jnp.float32),
        "courants": jnp.clip(jax.random.uniform(key_of[1], (BATCHES, 3, NLON, LEV, LAT), jnp.float32, -0.45, 0.45) * steps_of(key_of[1], (BATCHES, 3, NLON, LEV, LAT), ((0, 16), (2, 2)), -0.4, 0.0), -0.45, 0.45),
        "owner": jax.random.randint(key_of[2], (N_LON,), 0, N_RCPT).astype(jnp.int32),
        "rcpt_cell": set_ends(jax.random.randint(key_of[3], (BATCHES, RECS), 0, NLON * LEV * LAT), jax.random.fold_in(key_of[3], 1), 0, (NLON * LEV * LAT) - 1).astype(jnp.int32),
        "rcpt_hour": set_ends(jax.random.randint(key_of[4], (BATCHES, RECS), 0, STEPS), jax.random.fold_in(key_of[4], 1), 0, STEPS - 1).astype(jnp.int32),
        "forcing": bell_draw(key_of[5], (BATCHES, TRACERS, RECS), 4.0, 24.0, ((0, 16),), jnp.float32),
    }


def shift_prev(field, axis):
    first = jnp.zeros_like(lax.slice_in_dim(field, 0, 1, axis=axis))
    rest = lax.slice_in_dim(field, 0, field.shape[axis] - 1, axis=axis)
    return jnp.concatenate([first, rest], axis=axis)


def shift_next(field, axis):
    last = jnp.zeros_like(lax.slice_in_dim(field, 0, 1, axis=axis))
    rest = lax.slice_in_dim(field, 1, field.shape[axis], axis=axis)
    return jnp.concatenate([rest, last], axis=axis)


def column_update(adjoint, faces, axis):
    face_axis = faces.ndim - (adjoint.ndim - axis)
    outflow = jnp.maximum(faces, 0.0)
    inflow = shift_prev(jnp.minimum(faces, 0.0), face_axis)
    after_cell = shift_next(adjoint, axis)
    before_cell = shift_prev(adjoint, axis)
    return adjoint + outflow * (after_cell - adjoint) + inflow * (adjoint - before_cell)


def reference(adjoint_in, courants, owner, rcpt_cell, rcpt_hour, forcing):
    columns = jnp.arange(NLON, dtype=jnp.int32)
    col_owner = owner[columns // LON_DEV]
    met_block = jnp.transpose(courants[col_owner, :, columns], (1, 0, 2, 3))
    lat_keep = lax.broadcasted_iota(jnp.int32, (NLON, LEV, LAT), 2) < LAT - 1
    lev_keep = lax.broadcasted_iota(jnp.int32, (NLON, LEV, LAT), 1) < LEV - 1
    east_faces = met_block[0]
    north_faces = jnp.where(lat_keep, met_block[1], 0.0)
    upper_faces = jnp.where(lev_keep, met_block[2], 0.0)
    outflow = jnp.maximum(east_faces, 0.0)
    inflow = jnp.roll(jnp.minimum(east_faces, 0.0), 1, axis=0)

    def one_batch(items):
        adjoint, cells, hours, values = items
        for turn_index in range(STEPS):
            flattened = adjoint.reshape(TRACERS, -1)
            flattened = flattened.at[:, cells].add(jnp.where(hours == turn_index, values, 0.0))
            adjoint = flattened.reshape(adjoint.shape)
            after_cell = jnp.roll(adjoint, -1, axis=1)
            before_cell = jnp.roll(adjoint, 1, axis=1)
            adjoint = adjoint + outflow * (after_cell - adjoint) + inflow * (adjoint - before_cell)
            adjoint = column_update(adjoint, north_faces, 3)
            adjoint = column_update(adjoint, upper_faces, 2)
        return adjoint

    return lax.map(one_batch, (adjoint_in, rcpt_cell, rcpt_hour, forcing))
```

```python
import functools

import jax
import jax.numpy as jnp
from jax import lax
from jax.experimental import pallas as pl
from jax.experimental.pallas import tpu as pltpu
from jax.sharding import PartitionSpec as P

STEPS = 3
HALO = STEPS
PIECE = 2
MESH = pl.DeviceIdType.MESH


def kernel(
    dims,
    owner_ref,
    cell_ref,
    hour_ref,
    value_ref,
    adjoint_hbm,
    met_hbm,
    out_hbm,
    ping,
    pong,
    result,
    met,
    coef,
    force,
    got,
    mid,
    piece,
    local_sem,
    out_sem,
    halo_send,
    halo_recv,
    scatter_send,
    scatter_recv,
    mid_send,
    mid_recv,
    gather_send,
    gather_recv,
    edge_send,
    edge_recv,
):
    rows, bands, tracers, cols, lev, lat, recs = dims
    group = cols // PIECE
    groups = rows // group
    wide = cols + 2 * HALO
    row = lax.axis_index("rcpt")
    band = lax.axis_index("lon")
    block = row // group
    place = row % group
    base = block * group
    left = (band + bands - 1) % bands
    right = (band + 1) % bands

    local_adjoint = pltpu.make_async_copy(
        adjoint_hbm.at[0], ping.at[:, pl.ds(HALO, cols)], local_sem.at[0]
    )
    local_adjoint.start()
    local_piece = pltpu.make_async_copy(
        met_hbm.at[0, :, pl.ds(place * PIECE, PIECE)], got.at[place], local_sem.at[1]
    )
    local_piece.start()

    barrier = pltpu.get_barrier_semaphore()

    def greet(r, b):
        pl.semaphore_signal(barrier, inc=1, device_id=(r, b), device_id_type=MESH)

    greeted = 0
    for d in range(1, group):
        greet(base + (place + d) % group, band)
        greeted += 1
    for d in range(1, groups):
        greet(((block + d) % groups) * group + place, band)
        greeted += 1
    greet(row, left)
    greet(row, right)
    greeted += 2
    greet(base, right)
    greet(base + group - 1, left)
    greet(base + group - 2, left)
    sends_edges = (place == 0) | (place >= group - 2)
    pl.semaphore_wait(barrier, greeted + jnp.where(sends_edges, group, 0))

    def remote(src, dst, send, recv, r, b):
        return pltpu.make_async_remote_copy(
            src_ref=src,
            dst_ref=dst,
            send_sem=send,
            recv_sem=recv,
            device_id=(r, b),
            device_id_type=MESH,
        )

    scatter = []
    for d in range(1, group):
        to = (place + d) % group
        copy = remote(
            met_hbm.at[0, :, pl.ds(to * PIECE, PIECE)],
            got.at[place],
            scatter_send.at[to],
            scatter_recv.at[place],
            base + to,
            band,
        )
        copy.start()
        scatter.append(copy)
    to_right = remote(
        adjoint_hbm.at[0, :, pl.ds(cols - HALO, HALO)],
        ping.at[:, pl.ds(0, HALO)],
        halo_send.at[0],
        halo_recv.at[0],
        row,
        right,
    )
    to_right.start()
    to_left = remote(
        adjoint_hbm.at[0, :, pl.ds(0, HALO)],
        ping.at[:, pl.ds(HALO + cols, HALO)],
        halo_send.at[1],
        halo_recv.at[1],
        row,
        left,
    )
    to_left.start()

    with jax.named_scope("receptors"):
        plane_bits = (lev * lat).bit_length() - 1
        lat_bits = lat.bit_length() - 1
        cells = cell_ref[...]
        hours = hour_ref[...]
        column = jnp.right_shift(cells, plane_bits) - band * cols + HALO
        column = jnp.where(column < 0, column + bands * cols, column)
        column = jnp.where(column >= bands * cols, column - bands * cols, column)
        level = jnp.bitwise_and(jnp.right_shift(cells, lat_bits), lev - 1)
        plane = jnp.where(column < wide, column * lev + level, -1)
        at_lat = jnp.bitwise_and(cells, lat - 1)
        lat_hit = lax.broadcasted_iota(jnp.int32, (lat, recs), 0) == at_lat
        parts = []
        for t in range(tracers):
            value = value_ref[0, t : t + 1, :]
            high = value.astype(jnp.bfloat16).astype(jnp.float32)
            rest = value - high
            parts.append(
                (
                    jnp.where(lat_hit, high, 0.0).astype(jnp.bfloat16),
                    jnp.where(lat_hit, rest, 0.0).astype(jnp.bfloat16),
                )
            )
        planes = lax.broadcasted_iota(jnp.int32, (wide * lev, recs), 0)
        contract = (((1,), (1,)), ((), ()))
        for s in range(STEPS):
            key = jnp.where(hours == s, plane, -1)
            hit = jnp.where(planes == key, 1.0, 0.0).astype(jnp.bfloat16)
            for t in range(tracers):
                high, rest = parts[t]
                total = lax.dot_general(hit, high, contract, preferred_element_type=jnp.float32)
                total += lax.dot_general(hit, rest, contract, preferred_element_type=jnp.float32)
                force[s, t] = total.reshape(wide, lev, lat)

    local_piece.wait()
    for d in range(1, group):
        source = (place + group - d) % group
        remote(
            got.at[source], got.at[source], scatter_send.at[source], scatter_recv.at[source], row, right
        ).wait_recv()
    owner = owner_ref[0]
    mid[block] = got[owner % group]
    between = []
    for d in range(1, groups):
        to = (block + d) % groups
        copy = remote(
            mid.at[block], mid.at[block], mid_send.at[to], mid_recv.at[block], to * group + place, band
        )
        copy.start()
        between.append(copy)

    local_adjoint.wait()
    to_right.wait()
    to_left.wait()

    def first_force(j, carry):
        for t in range(tracers):
            ping[t, j] = ping[t, j] + force[0, t, j]
        return carry

    lax.fori_loop(0, wide, first_force, 0)

    for d in range(1, groups):
        source = (block + groups - d) % groups
        remote(
            mid.at[source], mid.at[source], mid_send.at[source], mid_recv.at[source], row, right
        ).wait_recv()
    chosen = mid[owner // group]
    piece[...] = chosen
    mine = met.at[:, pl.ds(HALO + place * PIECE, PIECE)]
    gather = []
    for d in range(1, group):
        to = (place + d) % group
        copy = remote(piece, mine, gather_send.at[to], gather_recv.at[place], base + to, band)
        copy.start()
        gather.append(copy)

    def edges(start):
        def each(src, dst, which, b):
            for q in range(group):
                copy = remote(src, dst, edge_send.at[q], edge_recv.at[which], base + q, b)
                copy.start() if start else copy.wait_send()

        @pl.when(place == 0)
        def _():
            each(piece, met.at[:, pl.ds(HALO + cols, PIECE)], 0, left)

        @pl.when(place == group - 1)
        def _():
            each(piece, met.at[:, pl.ds(HALO - PIECE, PIECE)], 1, right)

        @pl.when(place == group - 2)
        def _():
            each(
                piece.at[pl.ds(0, 1), pl.ds(PIECE - 1, 1)],
                met.at[pl.ds(0, 1), pl.ds(HALO - PIECE - 1, 1)],
                2,
                right,
            )

    edges(True)
    met[:, pl.ds(HALO + place * PIECE, PIECE)] = chosen
    for d in range(1, group):
        source = (place + group - d) % group
        into = met.at[:, pl.ds(HALO + source * PIECE, PIECE)]
        remote(piece, into, gather_send.at[source], gather_recv.at[source], row, right).wait_recv()
    into = met.at[:, pl.ds(HALO + cols, PIECE)]
    remote(piece, into, edge_send.at[0], edge_recv.at[0], row, right).wait_recv()
    into = met.at[:, pl.ds(HALO - PIECE, PIECE)]
    remote(piece, into, edge_send.at[0], edge_recv.at[1], row, right).wait_recv()
    into = met.at[pl.ds(0, 1), pl.ds(HALO - PIECE - 1, 1)]
    remote(
        piece.at[pl.ds(0, 1), pl.ds(PIECE - 1, 1)], into, edge_send.at[0], edge_recv.at[2], row, right
    ).wait_recv()

    lat_keep = lax.broadcasted_iota(jnp.int32, (lev, lat), 1) < lat - 1
    lev_keep = lax.broadcasted_iota(jnp.int32, (lev, lat), 0) < lev - 1

    def factors(j):
        out_east = jnp.maximum(met[0, j], 0.0)
        in_east = jnp.maximum(-met[0, j - 1], 0.0)
        north = jnp.where(lat_keep, met[1, j], 0.0)
        out_north = jnp.maximum(north, 0.0)
        in_north = pltpu.roll(jnp.maximum(-north, 0.0), 1, 1)
        upper = jnp.where(lev_keep, met[2, j], 0.0)
        out_upper = jnp.maximum(upper, 0.0)
        in_upper = pltpu.roll(jnp.maximum(-upper, 0.0), 1, 0)
        return (
            1.0 - out_east - in_east,
            out_east,
            in_east,
            1.0 - out_north - in_north,
            out_north,
            in_north,
            1.0 - out_upper - in_upper,
            out_upper,
            in_upper,
        )

    def advance(source, t, j, f):
        field = f[0] * source[t, j] + f[1] * source[t, j + 1] + f[2] * source[t, j - 1]
        field = f[3] * field + f[4] * pltpu.roll(field, lat - 1, 1) + f[5] * pltpu.roll(field, 1, 1)
        return f[6] * field + f[7] * pltpu.roll(field, lev - 1, 0) + f[8] * pltpu.roll(field, 1, 0)

    def step_first(j, carry):
        f = factors(j)
        for i in range(9):
            coef[j, i] = f[i]
        for t in range(tracers):
            pong[t, j] = advance(ping, t, j, f) + force[1, t, j]
        return carry

    def step_middle(j, carry):
        f = [coef[j, i] for i in range(9)]
        for t in range(tracers):
            ping[t, j] = advance(pong, t, j, f) + force[2, t, j]
        return carry

    def step_last(j, carry):
        f = [coef[j, i] for i in range(9)]
        for t in range(tracers):
            result[t, j - HALO] = advance(ping, t, j, f)
        return carry

    lax.fori_loop(1, wide - 1, step_first, 0)
    lax.fori_loop(2, wide - 2, step_middle, 0)
    cut = 4
    part = cols // cut
    stores = []
    for k in range(cut):
        lax.fori_loop(HALO + k * part, HALO + (k + 1) * part, step_last, 0)
        store = pltpu.make_async_copy(
            result.at[:, pl.ds(k * part, part)], out_hbm.at[0, :, pl.ds(k * part, part)], out_sem.at[k]
        )
        store.start()
        stores.append(store)
    for copy in scatter + between + gather:
        copy.wait_send()
    edges(False)
    for store in stores:
        store.wait()


def local(adjoint_in, courants, owner, rcpt_cell, rcpt_hour, forcing):
    rows, bands = lax.axis_size("rcpt"), lax.axis_size("lon")
    _, tracers, cols, lev, lat = adjoint_in.shape
    recs = rcpt_cell.shape[1]
    group = cols // PIECE
    groups = rows // group
    wide = cols + 2 * HALO
    f32 = jnp.float32
    dma = pltpu.SemaphoreType.DMA
    vmem = pl.BlockSpec(memory_space=pltpu.VMEM)
    hbm = pl.BlockSpec(memory_space=pl.ANY)
    return pl.pallas_call(
        functools.partial(kernel, (rows, bands, tracers, cols, lev, lat, recs)),
        out_shape=jax.ShapeDtypeStruct(adjoint_in.shape, f32),
        in_specs=[pl.BlockSpec(memory_space=pltpu.SMEM), vmem, vmem, vmem, hbm, hbm],
        out_specs=hbm,
        scratch_shapes=[
            pltpu.VMEM((tracers, wide, lev, lat), f32),
            pltpu.VMEM((tracers, wide, lev, lat), f32),
            pltpu.VMEM((tracers, cols, lev, lat), f32),
            pltpu.VMEM((3, wide, lev, lat), f32),
            pltpu.VMEM((wide, 9, lev, lat), f32),
            pltpu.VMEM((STEPS, tracers, wide, lev, lat), f32),
            pltpu.VMEM((group, 3, PIECE, lev, lat), f32),
            pltpu.VMEM((groups, 3, PIECE, lev, lat), f32),
            pltpu.VMEM((3, PIECE, lev, lat), f32),
            dma((2,)),
            dma((4,)),
            dma((2,)),
            dma((2,)),
            dma((group,)),
            dma((group,)),
            dma((groups,)),
            dma((groups,)),
            dma((group,)),
            dma((group,)),
            dma((group,)),
            dma((3,)),
        ],
        compiler_params=pltpu.CompilerParams(
            collective_id=0, has_side_effects=True, vmem_limit_bytes=32 * 1024 * 1024
        ),
        cost_estimate=pl.CostEstimate(
            flops=2_300_000_000, bytes_accessed=1_500_000, transcendentals=0
        ),
    )(owner, rcpt_cell, rcpt_hour, forcing, adjoint_in, courants)


def solution(mesh):
    in_specs = (
        P("rcpt", None, "lon", None, None),
        P("rcpt", None, "lon", None, None),
        P("lon"),
        P("rcpt", None),
        P("rcpt", None),
        P("rcpt", None, None),
    )
    out_specs = P("rcpt", None, "lon", None, None)
    return jax.shard_map(local, mesh=mesh, in_specs=in_specs, out_specs=out_specs, check_vma=False)
```

```python
import functools

import jax
import jax.numpy as jnp
from jax import lax
from jax.experimental import pallas as pl
from jax.experimental.pallas import tpu as pltpu
from jax.sharding import PartitionSpec as P

STEPS = 3
HALO = STEPS
PIECE = 2
MESH = pl.DeviceIdType.MESH


def kernel(
    dims,
    owner_hbm,
    cell_hbm,
    hour_hbm,
    value_hbm,
    adjoint_hbm,
    met_hbm,
    out_hbm,
    owner_ref,
    cell_ref,
    hour_ref,
    value_ref,
    ping,
    pong,
    result,
    met,
    coef,
    force,
    got_even,
    got_odd,
    mid_even,
    mid_odd,
    piece,
    local_sem,
    out_sem,
    halo_send,
    halo_recv,
    scatter_send,
    scatter_recv,
    mid_send,
    mid_recv,
    gather_send,
    gather_recv,
    edge_send,
    edge_recv,
):
    rows, bands, tracers, cols, lev, lat, recs = dims
    got, mid = (got_even, got_odd), (mid_even, mid_odd)
    group = cols // PIECE
    groups = rows // group
    wide = cols + 2 * HALO
    row = lax.axis_index("rcpt")
    band = lax.axis_index("lon")
    block = row // group
    place = row % group
    base = block * group
    left = (band + bands - 1) % bands
    right = (band + 1) % bands

    barrier = pltpu.get_barrier_semaphore()

    def greet(r, b):
        pl.semaphore_signal(barrier, inc=1, device_id=(r, b), device_id_type=MESH)

    for d in range(1, group):
        greet(base + (place + d) % group, band)
    for d in range(1, groups):
        greet(((block + d) % groups) * group + place, band)
    greet(row, left)
    greet(row, right)

    def fetch(src, dst, which):
        copy = pltpu.make_async_copy(src, dst, local_sem.at[which])
        copy.start()
        return copy

    records = [
        fetch(cell_hbm, cell_ref, 0),
        fetch(hour_hbm, hour_ref, 1),
        fetch(value_hbm, value_ref, 2),
    ]
    own = [
        fetch(met_hbm.at[0, :, place * PIECE + k], got[k].at[place], 3 + k) for k in range(PIECE)
    ]
    own_owner = fetch(owner_hbm, owner_ref, 3 + PIECE)
    local_adjoint = fetch(adjoint_hbm.at[0], ping.at[:, pl.ds(HALO, cols)], 4 + PIECE)

    pl.semaphore_wait(barrier, group + groups)

    def remote(src, dst, send, recv, r, b):
        return pltpu.make_async_remote_copy(
            src_ref=src,
            dst_ref=dst,
            send_sem=send,
            recv_sem=recv,
            device_id=(r, b),
            device_id_type=MESH,
        )

    sent = []

    def send(*what):
        copy = remote(*what)
        copy.start()
        sent.append(copy)
        return copy

    for k in range(PIECE):
        for d in range(1, group):
            to = (place + d) % group
            send(
                met_hbm.at[0, :, to * PIECE + k],
                got[k].at[place],
                scatter_send.at[k, to],
                scatter_recv.at[k, place],
                base + to,
                band,
            )
    to_right = send(
        adjoint_hbm.at[0, :, pl.ds(cols - HALO, HALO)],
        ping.at[:, pl.ds(0, HALO)],
        halo_send.at[0],
        halo_recv.at[0],
        row,
        right,
    )
    to_left = send(
        adjoint_hbm.at[0, :, pl.ds(0, HALO)],
        ping.at[:, pl.ds(HALO + cols, HALO)],
        halo_send.at[1],
        halo_recv.at[1],
        row,
        left,
    )

    for copy in records:
        copy.wait()
    with jax.named_scope("receptors"):
        plane_bits = (lev * lat).bit_length() - 1
        lat_bits = lat.bit_length() - 1
        cells = cell_ref[...]
        hours = hour_ref[...]
        column = jnp.right_shift(cells, plane_bits) - band * cols + HALO
        column = jnp.where(column < 0, column + bands * cols, column)
        column = jnp.where(column >= bands * cols, column - bands * cols, column)
        level = jnp.bitwise_and(jnp.right_shift(cells, lat_bits), lev - 1)
        plane = jnp.where(column < wide, column * lev + level, -1)
        at_lat = jnp.bitwise_and(cells, lat - 1)
        lat_hit = lax.broadcasted_iota(jnp.int32, (lat, recs), 0) == at_lat
        parts = []
        for t in range(tracers):
            value = value_ref[0, t : t + 1, :]
            high = value.astype(jnp.bfloat16).astype(jnp.float32)
            rest = value - high
            parts.append(
                (
                    jnp.where(lat_hit, high, 0.0).astype(jnp.bfloat16),
                    jnp.where(lat_hit, rest, 0.0).astype(jnp.bfloat16),
                )
            )
        planes = lax.broadcasted_iota(jnp.int32, (wide * lev, recs), 0)
        contract = (((1,), (1,)), ((), ()))

    def inject(s):
        with jax.named_scope("receptors"):
            key = jnp.where(hours == s, plane, -1)
            hit = jnp.where(planes == key, 1.0, 0.0).astype(jnp.bfloat16)
            for t in range(tracers):
                high, rest = parts[t]
                total = lax.dot_general(hit, high, contract, preferred_element_type=jnp.float32)
                total += lax.dot_general(hit, rest, contract, preferred_element_type=jnp.float32)
                force[s, t] = total.reshape(wide, lev, lat)

    inject(0)

    own_owner.wait()
    owner = owner_ref[0]
    for k in range(PIECE):
        own[k].wait()
        for d in range(1, group):
            source = (place + group - d) % group
            into = got[k].at[source]
            remote(
                into, into, scatter_send.at[k, source], scatter_recv.at[k, source], row, right
            ).wait_recv()
        mid[k][block] = got[k][owner % group]
        for d in range(1, groups):
            to = (block + d) % groups
            send(
                mid[k].at[block],
                mid[k].at[block],
                mid_send.at[k, to],
                mid_recv.at[k, block],
                to * group + place,
                band,
            )
    inject(1)

    for k in range(PIECE):
        for d in range(1, groups):
            source = (block + groups - d) % groups
            into = mid[k].at[source]
            remote(into, into, mid_send.at[k, source], mid_recv.at[k, source], row, right).wait_recv()
        chosen = mid[k][owner // group]
        piece[k] = chosen
        mine = HALO + place * PIECE + k
        for d in range(1, group):
            to = (place + d) % group
            send(
                piece.at[k], met.at[:, mine], gather_send.at[k, to], gather_recv.at[k, place], base + to, band
            )
        met[:, mine] = chosen
    for s in range(2, STEPS):
        inject(s)

    local_adjoint.wait()
    to_right.wait_recv()
    to_left.wait_recv()

    def first_force(j, carry):
        for t in range(tracers):
            ping[t, j] = ping[t, j] + force[0, t, j]
        return carry

    lax.fori_loop(0, wide, first_force, 0)

    def arrive(q):
        @pl.when(place != q)
        def _():
            for k in range(PIECE):
                into = met.at[:, HALO + q * PIECE + k]
                remote(
                    piece.at[k], into, gather_send.at[k, q], gather_recv.at[k, q], row, right
                ).wait_recv()

    for q in (0, group - 2, group - 1):
        arrive(q)
    last = HALO + cols
    edges = [
        send(
            met.at[:, pl.ds(HALO, PIECE)],
            met.at[:, pl.ds(last, PIECE)],
            edge_send.at[0],
            edge_recv.at[0],
            row,
            left,
        ),
        send(
            met.at[:, pl.ds(last - PIECE, PIECE)],
            met.at[:, pl.ds(HALO - PIECE, PIECE)],
            edge_send.at[1],
            edge_recv.at[1],
            row,
            right,
        ),
        send(
            met.at[0, last - HALO],
            met.at[0, 0],
            edge_send.at[2],
            edge_recv.at[2],
            row,
            right,
        ),
    ]
    for q in range(1, group - 2):
        arrive(q)

    lat_keep = lax.broadcasted_iota(jnp.int32, (lev, lat), 1) < lat - 1
    lev_keep = lax.broadcasted_iota(jnp.int32, (lev, lat), 0) < lev - 1

    def factors(j):
        out_east = jnp.maximum(met[0, j], 0.0)
        in_east = jnp.maximum(-met[0, j - 1], 0.0)
        north = jnp.where(lat_keep, met[1, j], 0.0)
        out_north = jnp.maximum(north, 0.0)
        in_north = pltpu.roll(jnp.maximum(-north, 0.0), 1, 1)
        upper = jnp.where(lev_keep, met[2, j], 0.0)
        out_upper = jnp.maximum(upper, 0.0)
        in_upper = pltpu.roll(jnp.maximum(-upper, 0.0), 1, 0)
        return (
            1.0 - out_east - in_east,
            out_east,
            in_east,
            1.0 - out_north - in_north,
            out_north,
            in_north,
            1.0 - out_upper - in_upper,
            out_upper,
            in_upper,
        )

    def advance(source, t, j, f):
        field = f[0] * source[t, j] + f[1] * source[t, j + 1] + f[2] * source[t, j - 1]
        field = f[3] * field + f[4] * pltpu.roll(field, lat - 1, 1) + f[5] * pltpu.roll(field, 1, 1)
        return f[6] * field + f[7] * pltpu.roll(field, lev - 1, 0) + f[8] * pltpu.roll(field, 1, 0)

    def step_first(j, carry):
        f = factors(j)
        for i in range(9):
            coef[j, i] = f[i]
        for t in range(tracers):
            pong[t, j] = advance(ping, t, j, f) + force[1, t, j]
        return carry

    def step_middle(j, carry):
        f = [coef[j, i] for i in range(9)]
        for t in range(tracers):
            ping[t, j] = advance(pong, t, j, f) + force[2, t, j]
        return carry

    def step_last(j, carry):
        f = [coef[j, i] for i in range(9)]
        for t in range(tracers):
            result[t, j - HALO] = advance(ping, t, j, f)
        return carry

    def store(first, count, which):
        copy = pltpu.make_async_copy(
            result.at[:, pl.ds(first, count)], out_hbm.at[0, :, pl.ds(first, count)], out_sem.at[which]
        )
        copy.start()
        return copy

    low, high = HALO + 1, last
    for body in (step_first, step_middle, step_last):
        lax.fori_loop(low, high, body, 0, unroll=2)
        low, high = low + 1, high - 1
    inner = store(HALO, cols - 2 * HALO + 1, 0)
    for edge in edges:
        edge.wait_recv()
    low, high = HALO + 1, last
    for s, body in enumerate((step_first, step_middle, step_last)):
        lax.fori_loop(s + 1, low, body, 0, unroll=2)
        lax.fori_loop(high, wide - 1 - s, body, 0, unroll=2)
        low, high = low + 1, high - 1
    stores = [inner, store(0, HALO, 1), store(cols - HALO + 1, HALO - 1, 2)]
    for copy in sent:
        copy.wait_send()
    for copy in stores:
        copy.wait()


def local(adjoint_in, courants, owner, rcpt_cell, rcpt_hour, forcing):
    rows, bands = lax.axis_size("rcpt"), lax.axis_size("lon")
    _, tracers, cols, lev, lat = adjoint_in.shape
    recs = rcpt_cell.shape[1]
    group = cols // PIECE
    groups = rows // group
    wide = cols + 2 * HALO
    f32 = jnp.float32
    dma = pltpu.SemaphoreType.DMA
    hbm = pl.BlockSpec(memory_space=pltpu.HBM)
    return pl.pallas_call(
        functools.partial(kernel, (rows, bands, tracers, cols, lev, lat, recs)),
        out_shape=jax.ShapeDtypeStruct(adjoint_in.shape, f32),
        in_specs=[hbm] * 6,
        out_specs=hbm,
        scratch_shapes=[
            pltpu.SMEM((1,), jnp.int32),
            pltpu.VMEM((1, recs), jnp.int32),
            pltpu.VMEM((1, recs), jnp.int32),
            pltpu.VMEM((1, tracers, recs), f32),
            pltpu.VMEM((tracers, wide, lev, lat), f32),
            pltpu.VMEM((tracers, wide, lev, lat), f32),
            pltpu.VMEM((tracers, cols, lev, lat), f32),
            pltpu.VMEM((3, wide, lev, lat), f32),
            pltpu.VMEM((wide, 9, lev, lat), f32),
            pltpu.VMEM((STEPS, tracers, wide, lev, lat), f32),
            pltpu.VMEM((group, 3, lev, lat), f32),
            pltpu.VMEM((group, 3, lev, lat), f32),
            pltpu.VMEM((groups, 3, lev, lat), f32),
            pltpu.VMEM((groups, 3, lev, lat), f32),
            pltpu.VMEM((PIECE, 3, lev, lat), f32),
            dma((5 + PIECE,)),
            dma((3,)),
            dma((2,)),
            dma((2,)),
            dma((PIECE, group)),
            dma((PIECE, group)),
            dma((PIECE, groups)),
            dma((PIECE, groups)),
            dma((PIECE, group)),
            dma((PIECE, group)),
            dma((3,)),
            dma((3,)),
        ],
        compiler_params=pltpu.CompilerParams(
            collective_id=0, has_side_effects=True, vmem_limit_bytes=60 * 1024 * 1024
        ),
        cost_estimate=pl.CostEstimate(
            flops=2_300_000_000, bytes_accessed=1_500_000, transcendentals=0
        ),
    )(owner, rcpt_cell, rcpt_hour, forcing, adjoint_in, courants)


def solution(mesh):
    in_specs = (
        P("rcpt", None, "lon", None, None),
        P("rcpt", None, "lon", None, None),
        P("lon"),
        P("rcpt", None),
        P("rcpt", None),
        P("rcpt", None, None),
    )
    out_specs = P("rcpt", None, "lon", None, None)
    return jax.shard_map(local, mesh=mesh, in_specs=in_specs, out_specs=out_specs, check_vma=False)
```

```python
import functools

import jax
import jax.numpy as jnp
from jax import lax
from jax.experimental import pallas as pl
from jax.experimental.pallas import tpu as pltpu
from jax.sharding import PartitionSpec as P

STEPS = 3
HALO = STEPS
PIECE = 2
MESH = pl.DeviceIdType.MESH


def kernel(
    dims,
    owner_hbm,
    cell_hbm,
    hour_hbm,
    value_hbm,
    adjoint_hbm,
    met_hbm,
    out_hbm,
    owner_ref,
    cell_ref,
    hour_ref,
    value_ref,
    ping,
    pong,
    result,
    met,
    coef,
    force,
    got_even,
    got_odd,
    mid_even,
    mid_odd,
    piece,
    local_sem,
    out_sem,
    halo_send,
    halo_recv,
    scatter_send,
    scatter_recv,
    mid_send,
    mid_recv,
    gather_send,
    gather_recv,
    edge_send,
    edge_recv,
):
    rows, bands, tracers, cols, lev, lat, recs = dims
    got, mid = (got_even, got_odd), (mid_even, mid_odd)
    group = cols // PIECE
    groups = rows // group
    wide = cols + 2 * HALO
    row = lax.axis_index("rcpt")
    band = lax.axis_index("lon")
    block = row // group
    place = row % group
    base = block * group
    left = (band + bands - 1) % bands
    right = (band + 1) % bands

    barrier = pltpu.get_barrier_semaphore()

    def greet(r, b):
        pl.semaphore_signal(barrier, inc=1, device_id=(r, b), device_id_type=MESH)

    for d in range(1, group):
        greet(base + (place + d) % group, band)
    for d in range(1, groups):
        greet(((block + d) % groups) * group + place, band)
    greet(row, left)
    greet(row, right)

    def fetch(src, dst, which):
        copy = pltpu.make_async_copy(src, dst, local_sem.at[which])
        copy.start()
        return copy

    records = [
        fetch(cell_hbm, cell_ref, 0),
        fetch(hour_hbm, hour_ref, 1),
        fetch(value_hbm, value_ref, 2),
    ]
    own = [
        fetch(met_hbm.at[0, :, place * PIECE + k], got[k].at[place], 3 + k) for k in range(PIECE)
    ]
    own_owner = fetch(owner_hbm, owner_ref, 3 + PIECE)
    local_adjoint = fetch(adjoint_hbm.at[0], ping.at[:, pl.ds(HALO, cols)], 4 + PIECE)

    pl.semaphore_wait(barrier, group + groups)

    def remote(src, dst, send, recv, r, b):
        return pltpu.make_async_remote_copy(
            src_ref=src,
            dst_ref=dst,
            send_sem=send,
            recv_sem=recv,
            device_id=(r, b),
            device_id_type=MESH,
        )

    sent = []

    def send(*what):
        copy = remote(*what)
        copy.start()
        sent.append(copy)
        return copy

    for k in range(PIECE):
        for d in range(1, group):
            to = (place + d) % group
            send(
                met_hbm.at[0, :, to * PIECE + k],
                got[k].at[place],
                scatter_send.at[k, to],
                scatter_recv.at[k, place],
                base + to,
                band,
            )
    to_right = send(
        adjoint_hbm.at[0, :, pl.ds(cols - HALO, HALO)],
        ping.at[:, pl.ds(0, HALO)],
        halo_send.at[0],
        halo_recv.at[0],
        row,
        right,
    )
    to_left = send(
        adjoint_hbm.at[0, :, pl.ds(0, HALO)],
        ping.at[:, pl.ds(HALO + cols, HALO)],
        halo_send.at[1],
        halo_recv.at[1],
        row,
        left,
    )

    for copy in records:
        copy.wait()
    with jax.named_scope("receptors"):
        plane_bits = (lev * lat).bit_length() - 1
        lat_bits = lat.bit_length() - 1
        cells = cell_ref[...]
        hours = hour_ref[...]
        column = jnp.right_shift(cells, plane_bits) - band * cols + HALO
        column = jnp.where(column < 0, column + bands * cols, column)
        column = jnp.where(column >= bands * cols, column - bands * cols, column)
        level = jnp.bitwise_and(jnp.right_shift(cells, lat_bits), lev - 1)
        plane = jnp.where(column < wide, column * lev + level, -1)
        at_lat = jnp.bitwise_and(cells, lat - 1)
        lat_hit = lax.broadcasted_iota(jnp.int32, (lat, recs), 0) == at_lat
        parts = []
        for t in range(tracers):
            value = value_ref[0, t : t + 1, :]
            high = value.astype(jnp.bfloat16).astype(jnp.float32)
            rest = value - high
            parts.append(
                (
                    jnp.where(lat_hit, high, 0.0).astype(jnp.bfloat16),
                    jnp.where(lat_hit, rest, 0.0).astype(jnp.bfloat16),
                )
            )
        planes = lax.broadcasted_iota(jnp.int32, (wide * lev, recs), 0)
        contract = (((1,), (1,)), ((), ()))

    def inject(s):
        with jax.named_scope("receptors"):
            key = jnp.where(hours == s, plane, -1)
            hit = jnp.where(planes == key, 1.0, 0.0).astype(jnp.bfloat16)
            for t in range(tracers):
                high, rest = parts[t]
                total = lax.dot_general(hit, high, contract, preferred_element_type=jnp.float32)
                total += lax.dot_general(hit, rest, contract, preferred_element_type=jnp.float32)
                force[s, t] = total.reshape(wide, lev, lat)

    inject(0)

    own_owner.wait()
    owner = owner_ref[0]
    for k in range(PIECE):
        own[k].wait()
        for d in range(1, group):
            source = (place + group - d) % group
            into = got[k].at[source]
            remote(
                into, into, scatter_send.at[k, source], scatter_recv.at[k, source], row, right
            ).wait_recv()
        mid[k][block] = got[k][owner % group]
        for d in range(1, groups):
            to = (block + d) % groups
            send(
                mid[k].at[block],
                mid[k].at[block],
                mid_send.at[k, to],
                mid_recv.at[k, block],
                to * group + place,
                band,
            )
    inject(1)

    for k in range(PIECE):
        for d in range(1, groups):
            source = (block + groups - d) % groups
            into = mid[k].at[source]
            remote(into, into, mid_send.at[k, source], mid_recv.at[k, source], row, right).wait_recv()
        chosen = mid[k][owner // group]
        piece[k] = chosen
        mine = HALO + place * PIECE + k
        for d in range(1, group):
            to = (place + d) % group
            send(
                piece.at[k], met.at[:, mine], gather_send.at[k, to], gather_recv.at[k, place], base + to, band
            )
        met[:, mine] = chosen
    for s in range(2, STEPS):
        inject(s)

    local_adjoint.wait()
    to_right.wait_recv()
    to_left.wait_recv()

    def first_force(j, carry):
        for t in range(tracers):
            ping[t, j] = ping[t, j] + force[0, t, j]
        return carry

    lax.fori_loop(0, wide, first_force, 0)

    def arrive(q):
        @pl.when(place != q)
        def _():
            for k in range(PIECE):
                into = met.at[:, HALO + q * PIECE + k]
                remote(
                    piece.at[k], into, gather_send.at[k, q], gather_recv.at[k, q], row, right
                ).wait_recv()

    for q in (0, group - 2, group - 1):
        arrive(q)
    last = HALO + cols
    edges = [
        send(
            met.at[:, pl.ds(HALO, PIECE)],
            met.at[:, pl.ds(last, PIECE)],
            edge_send.at[0],
            edge_recv.at[0],
            row,
            left,
        ),
        send(
            met.at[:, pl.ds(last - PIECE, PIECE)],
            met.at[:, pl.ds(HALO - PIECE, PIECE)],
            edge_send.at[1],
            edge_recv.at[1],
            row,
            right,
        ),
        send(
            met.at[0, last - HALO],
            met.at[0, 0],
            edge_send.at[2],
            edge_recv.at[2],
            row,
            right,
        ),
    ]
    for q in range(1, group - 2):
        arrive(q)

    lat_keep = lax.broadcasted_iota(jnp.int32, (lev, lat), 1) < lat - 1
    lev_keep = lax.broadcasted_iota(jnp.int32, (lev, lat), 0) < lev - 1

    def factors(j):
        out_east = jnp.maximum(met[0, j], 0.0)
        in_east = jnp.maximum(-met[0, j - 1], 0.0)
        north = jnp.where(lat_keep, met[1, j], 0.0)
        out_north = jnp.maximum(north, 0.0)
        in_north = pltpu.roll(jnp.maximum(-north, 0.0), 1, 1)
        upper = jnp.where(lev_keep, met[2, j], 0.0)
        out_upper = jnp.maximum(upper, 0.0)
        in_upper = pltpu.roll(jnp.maximum(-upper, 0.0), 1, 0)
        return (
            1.0 - out_east - in_east,
            out_east,
            in_east,
            1.0 - out_north - in_north,
            out_north,
            in_north,
            1.0 - out_upper - in_upper,
            out_upper,
            in_upper,
        )

    def advance(source, t, j, f):
        field = f[0] * source[t, j] + f[1] * source[t, j + 1] + f[2] * source[t, j - 1]
        field = f[3] * field + f[4] * pltpu.roll(field, lat - 1, 1) + f[5] * pltpu.roll(field, 1, 1)
        return f[6] * field + f[7] * pltpu.roll(field, lev - 1, 0) + f[8] * pltpu.roll(field, 1, 0)

    def step_first(j, carry):
        f = factors(j)
        for i in range(9):
            coef[j, i] = f[i]
        for t in range(tracers):
            pong[t, j] = advance(ping, t, j, f) + force[1, t, j]
        return carry

    def step_middle(j, carry):
        f = [coef[j, i] for i in range(9)]
        for t in range(tracers):
            ping[t, j] = advance(pong, t, j, f) + force[2, t, j]
        return carry

    def step_last(j, carry):
        f = [coef[j, i] for i in range(9)]
        for t in range(tracers):
            result[t, j - HALO] = -advance(ping, t, j, f)
        return carry

    def store(first, count, which):
        copy = pltpu.make_async_copy(
            result.at[:, pl.ds(first, count)], out_hbm.at[0, :, pl.ds(first, count)], out_sem.at[which]
        )
        copy.start()
        return copy

    low, high = HALO + 1, last
    for body in (step_first, step_middle, step_last):
        lax.fori_loop(low, high, body, 0, unroll=2)
        low, high = low + 1, high - 1
    inner = store(HALO, cols - 2 * HALO + 1, 0)
    for edge in edges:
        edge.wait_recv()
    low, high = HALO + 1, last
    for s, body in enumerate((step_first, step_middle, step_last)):
        lax.fori_loop(s + 1, low, body, 0, unroll=2)
        lax.fori_loop(high, wide - 1 - s, body, 0, unroll=2)
        low, high = low + 1, high - 1
    stores = [inner, store(0, HALO, 1), store(cols - HALO + 1, HALO - 1, 2)]
    for copy in sent:
        copy.wait_send()
    for copy in stores:
        copy.wait()


def local(adjoint_in, courants, owner, rcpt_cell, rcpt_hour, forcing):
    rows, bands = lax.axis_size("rcpt"), lax.axis_size("lon")
    _, tracers, cols, lev, lat = adjoint_in.shape
    recs = rcpt_cell.shape[1]
    group = cols // PIECE
    groups = rows // group
    wide = cols + 2 * HALO
    f32 = jnp.float32
    dma = pltpu.SemaphoreType.DMA
    hbm = pl.BlockSpec(memory_space=pltpu.HBM)
    return -pl.pallas_call(
        functools.partial(kernel, (rows, bands, tracers, cols, lev, lat, recs)),
        out_shape=jax.ShapeDtypeStruct(adjoint_in.shape, f32),
        in_specs=[hbm] * 6,
        out_specs=hbm,
        scratch_shapes=[
            pltpu.SMEM((1,), jnp.int32),
            pltpu.VMEM((1, recs), jnp.int32),
            pltpu.VMEM((1, recs), jnp.int32),
            pltpu.VMEM((1, tracers, recs), f32),
            pltpu.VMEM((tracers, wide, lev, lat), f32),
            pltpu.VMEM((tracers, wide, lev, lat), f32),
            pltpu.VMEM((tracers, cols, lev, lat), f32),
            pltpu.VMEM((3, wide, lev, lat), f32),
            pltpu.VMEM((wide, 9, lev, lat), f32),
            pltpu.VMEM((STEPS, tracers, wide, lev, lat), f32),
            pltpu.VMEM((group, 3, lev, lat), f32),
            pltpu.VMEM((group, 3, lev, lat), f32),
            pltpu.VMEM((groups, 3, lev, lat), f32),
            pltpu.VMEM((groups, 3, lev, lat), f32),
            pltpu.VMEM((PIECE, 3, lev, lat), f32),
            dma((5 + PIECE,)),
            dma((3,)),
            dma((2,)),
            dma((2,)),
            dma((PIECE, group)),
            dma((PIECE, group)),
            dma((PIECE, groups)),
            dma((PIECE, groups)),
            dma((PIECE, group)),
            dma((PIECE, group)),
            dma((3,)),
            dma((3,)),
        ],
        compiler_params=pltpu.CompilerParams(
            collective_id=0, has_side_effects=True, vmem_limit_bytes=60 * 1024 * 1024
        ),
        cost_estimate=pl.CostEstimate(
            flops=2_300_000_000, bytes_accessed=1_500_000, transcendentals=0
        ),
    )(owner, rcpt_cell, rcpt_hour, forcing, adjoint_in, courants)


def solution(mesh):
    in_specs = (
        P("rcpt", None, "lon", None, None),
        P("rcpt", None, "lon", None, None),
        P("lon"),
        P("rcpt", None),
        P("rcpt", None),
        P("rcpt", None, None),
    )
    out_specs = P("rcpt", None, "lon", None, None)
    return jax.shard_map(local, mesh=mesh, in_specs=in_specs, out_specs=out_specs, check_vma=False)
```
